32 devices in a mesh: row: 32 (over z, y, x, core).
Axes of the slice: x: 2, y: 2, z: 4, core: 2. Of those that a mesh axis runs over, the one named last changes fastest.
Arguments:
- aux_slab: float32 [768, 16384], P(None, 'row'), may hold values from -0.21875 to 0.21875
- gaps: float32 [768], replicated, may hold values from 0.1 to 10
- frequency: float32 [1], replicated, may hold values from 0.1 to 10
Outputs:
- cyclic_matrix: float32 [32, 2048, 4096], P('row')
The draws below stay inside these ranges and needn't reach their ends.
All inputs are finite; a program needn't handle non-finite values.
Results may differ from the reference program's by a relative error of at most 0.00005.
Values sent between devices are 32-bit elements; how exact they have to be, the bound alone decides.
A program may use at most 192 MiB of HBM per device.

```python
import math
import jax
import jax.numpy as jnp
from jax import lax

NAUX = 16384
ROWS = 768
PC = 4
PR = 8
BLOCK = 512
N_ROW = 32


def level_of(rng, shape, cuts, smallest, top_value):
    level = 1.0
    for dim, parts in cuts:
        steps = jax.random.uniform(jax.random.fold_in(jax.random.fold_in(rng, 6), dim), (parts,), jnp.float32, smallest / len(cuts), top_value / len(cuts))
        level = level * jnp.repeat(jnp.exp(steps), shape[dim] // parts).reshape((-1,) + (1,) * (len(shape) - 1 - dim))
    return level


def noise(rng, shape, deviation, bound, split=(), held_as=jnp.bfloat16):
    result = deviation * jax.random.normal(rng, shape, jnp.float32)
    if split:
        result = result * level_of(rng, shape, split, -0.22, 0.18)
    return jnp.clip(result, -bound, bound).astype(held_as)


def setup_inputs(seed: int = 0) -> dict:
    arg_keys = jax.random.split(jax.random.key(seed), 4)
    aux_slab = noise(arg_keys[0], (ROWS, NAUX), ROWS ** -0.5, 0.21875, ((1, 32),), jnp.float32)
    gaps = jnp.clip(jnp.exp(jax.random.uniform(arg_keys[1], (ROWS,), jnp.float32, math.log(0.1), math.log(10.0))), 0.1, 10.0)
    frequency = jnp.clip(jnp.exp(jax.random.uniform(arg_keys[2], (1,), jnp.float32, math.log(0.1), math.log(10.0))), 0.1, 10.0)
    return dict(aux_slab=aux_slab, gaps=gaps, frequency=frequency)


def reference(aux_slab, gaps, frequency):
    weights = 2.0 * gaps / (gaps * gaps + frequency[0] * frequency[0])
    weighted = aux_slab * weights[:, None]
    coupling = lax.dot_general(weighted, aux_slab, (((0,), (0,)), ((), ())), precision=lax.Precision.HIGHEST, preferred_element_type=jnp.float32)
    coupling = coupling + jnp.eye(NAUX, dtype=jnp.float32)
    shaped = coupling.reshape(PC, PR, BLOCK, PR, PC, BLOCK).transpose(1, 4, 0, 2, 3, 5)
    return shaped.reshape(N_ROW, PC * BLOCK, PR * BLOCK)
```

```python
import functools
import jax
import jax.numpy as jnp
from jax import lax
from jax.experimental import pallas as pl
from jax.experimental.pallas import tpu as pltpu
from jax.sharding import PartitionSpec as P

MESH = pl.DeviceIdType.MESH
CHUNKS = 4
LAG = 2


def slot_at(place, grid_rows):
    place = lax.rem(place + 2 * grid_rows, grid_rows)
    return jnp.where(place < grid_rows // 2, 2 * place, 2 * (grid_rows - 1 - place) + 1)


def place_of(slot, grid_rows):
    return jnp.where(lax.rem(slot, 2) == 0, slot // 2, grid_rows - 1 - slot // 2)


def flipped(value, weight):
    return value + weight * (1 - 2 * lax.rem(value // weight, 2))


def gather_kernel(
    grid_rows, grid_cols, block_ref, col_ref, row_ref, own_sem, keep_sem, ring_send, ring_recv, row_send, row_recv
):
    bits = grid_cols.bit_length() - 1
    half = grid_rows // 2
    depth = block_ref.shape[0] // CHUNKS
    spread = grid_rows // grid_cols
    me = lax.axis_index("row")
    grid_row, grid_col = me // grid_cols, lax.rem(me, grid_cols)
    source_col = lax.rem(grid_row, grid_cols)
    place = place_of(grid_row, grid_rows)
    right = slot_at(place + 1, grid_rows) * grid_cols + grid_col
    left = slot_at(place - 1, grid_rows) * grid_cols + grid_col
    neighbours = (right, left)
    differs = [
        lax.rem(grid_col // 2**bit + source_col // 2**bit, 2) for bit in range(bits)
    ]
    none_below = [jnp.int32(1)]
    for bit in range(bits):
        none_below.append(none_below[-1] * (1 - differs[bit]))
    is_source = none_below[bits] == 1
    passes = [none_below[bit + 1] == 1 for bit in range(bits)]
    children = [grid_row * grid_cols + flipped(grid_col, 2**bit) for bit in range(bits)]

    own_copy = pltpu.make_async_copy(block_ref, col_ref.at[grid_row], own_sem)
    own_copy.start()
    barrier = pltpu.get_barrier_semaphore()
    for dev in (right, left):
        pl.semaphore_signal(barrier, inc=1, device_id=(dev,), device_id_type=MESH)
    for step in range(1, grid_cols):
        dev = grid_row * grid_cols + lax.rem(grid_col + step, grid_cols)
        pl.semaphore_signal(barrier, inc=1, device_id=(dev,), device_id_type=MESH)
    pl.semaphore_wait(barrier, 1 + grid_cols)
    own_copy.wait()

    def chunk(ref, slot, part):
        return ref.at[slot, pl.ds(pl.multiple_of(part * depth, 8), depth), :]

    def ring_copy(way, slot, step, part):
        return pltpu.make_async_remote_copy(
            src_ref=chunk(col_ref, slot, part),
            dst_ref=chunk(col_ref, slot, part),
            send_sem=ring_send.at[way, step, part],
            recv_sem=ring_recv.at[way, step, part],
            device_id=(neighbours[way],),
            device_id_type=MESH,
        )

    def row_copy(ref, slot, row_slot, part, bit):
        return pltpu.make_async_remote_copy(
            src_ref=chunk(ref, slot, part),
            dst_ref=chunk(row_ref, row_slot, part),
            send_sem=row_send.at[bit, row_slot, part],
            recv_sem=row_recv.at[row_slot, part],
            device_id=(children[bit],),
            device_id_type=MESH,
        )

    def keep_copy(slot, row_slot, part):
        return pltpu.make_async_copy(
            chunk(col_ref, slot, part), chunk(row_ref, row_slot, part), keep_sem.at[row_slot, part]
        )

    def event(index):
        step, turn = index // CHUNKS, lax.rem(index, CHUNKS)
        ways = []
        for way, part in ((0, turn), (1, CHUNKS - 1 - turn)):
            slot = slot_at(place - step if way == 0 else place + step, grid_rows)
            sends = (step < half - 1) | ((step == half - 1) & (turn < CHUNKS // 2))
            counts = (step > 0) if way == 1 else (step >= 0)
            in_row = counts & (lax.rem(slot, spread) == grid_row // grid_cols)
            ways.append((way, part, slot, slot // spread, step, sends, in_row))
        return ways

    total = half * CHUNKS + CHUNKS // 2

    def arrive(index):
        for way, part, slot, row_slot, step, sends, in_row in event(index):

            @pl.when(step > 0)
            def _():
                ring_copy(way, slot, step - 1, part).wait_recv()

            @pl.when(sends)
            def _():
                ring_copy(way, slot, step, part).start()

            @pl.when(in_row & is_source)
            def _():
                for bit in range(bits - 1, -1, -1):
                    row_copy(col_ref, slot, row_slot, part, bit).start()
                keep_copy(slot, row_slot, part).start()

    def relay(index):
        for way, part, slot, row_slot, step, sends, in_row in event(index):

            @pl.when(in_row & jnp.logical_not(is_source))
            def _():
                row_copy(col_ref, slot, row_slot, part, 0).wait_recv()
                for bit in range(bits - 1, -1, -1):

                    @pl.when(passes[bit])
                    def _():
                        row_copy(row_ref, row_slot, row_slot, part, bit).start()

    def drain(index):
        for way, part, slot, row_slot, step, sends, in_row in event(index):

            @pl.when(sends)
            def _():
                ring_copy(way, slot, step, part).wait_send()

            for bit in range(bits):

                @pl.when(in_row & passes[bit])
                def _():
                    row_copy(col_ref, slot, row_slot, part, bit).wait_send()

            @pl.when(in_row & is_source)
            def _():
                keep_copy(slot, row_slot, part).wait()

    @pl.loop(0, total + LAG)
    def _(index):
        @pl.when(index < total)
        def _():
            arrive(index)

        @pl.when(index >= LAG)
        def _():
            relay(index - LAG)

    @pl.loop(0, total)
    def _(index):
        drain(index)


def gather_panels(block, grid_rows, grid_cols):
    bits = grid_cols.bit_length() - 1
    half = grid_rows // 2
    return pl.pallas_call(
        functools.partial(gather_kernel, grid_rows, grid_cols),
        out_shape=[
            jax.ShapeDtypeStruct((grid_rows, *block.shape), jnp.float32),
            jax.ShapeDtypeStruct((grid_cols, *block.shape), jnp.float32),
        ],
        in_specs=[pl.BlockSpec(memory_space=pl.ANY)],
        out_specs=[pl.BlockSpec(memory_space=pl.ANY)] * 2,
        scratch_shapes=[
            pltpu.SemaphoreType.DMA,
            pltpu.SemaphoreType.DMA((grid_cols, CHUNKS)),
            pltpu.SemaphoreType.DMA((2, half, CHUNKS)),
            pltpu.SemaphoreType.DMA((2, half, CHUNKS)),
            pltpu.SemaphoreType.DMA((bits, grid_cols, CHUNKS)),
            pltpu.SemaphoreType.DMA((grid_cols, CHUNKS)),
        ],
        compiler_params=pltpu.CompilerParams(collective_id=0, has_side_effects=True),
        name="gather_panels",
    )(block)


def split(value):
    high = value.astype(jnp.bfloat16)
    return high, (value - high.astype(jnp.float32)).astype(jnp.bfloat16)


def product_kernel(grid_rows, grid_cols, row_ref, col_ref, out_ref, row_high, row_low, col_high, col_low):
    u, v = pl.program_id(0), pl.program_id(1)
    me = lax.axis_index("row")
    grid_row, grid_col = me // grid_cols, lax.rem(me, grid_cols)

    @pl.when(v == 0)
    def _():
        high, low = split(row_ref[0].T)
        row_high[...] = high
        row_low[...] = low

    @pl.when(u == 0)
    def _():
        high, low = split(col_ref[0])
        col_high[v] = high
        col_low[v] = low

    def dot(left, right):
        return jnp.dot(left[...], right, preferred_element_type=jnp.float32)

    out_ref[...] = dot(row_high, col_high[v]) + (dot(row_high, col_low[v]) + dot(row_low, col_high[v]))

    @pl.when(u * grid_rows + grid_row == v * grid_cols + grid_col)
    def _():
        width = out_ref.shape[0]
        lines = lax.broadcasted_iota(jnp.int32, (width, width), 0)
        lanes = lax.broadcasted_iota(jnp.int32, (width, width), 1)
        out_ref[...] += (lines == lanes).astype(jnp.float32)


def product(row_panel, col_panel):
    grid_cols, rows, width = row_panel.shape
    grid_rows = col_panel.shape[0]
    return pl.pallas_call(
        functools.partial(product_kernel, grid_rows, grid_cols),
        grid=(grid_cols, grid_rows),
        in_specs=[
            pl.BlockSpec((1, rows, width), lambda u, v: (u, 0, 0)),
            pl.BlockSpec((1, rows, width), lambda u, v: (jnp.where(u == 0, v, grid_rows - 1), 0, 0)),
        ],
        out_specs=pl.BlockSpec((width, width), lambda u, v: (u, v)),
        out_shape=jax.ShapeDtypeStruct((grid_cols * width, grid_rows * width), jnp.float32),
        scratch_shapes=[
            pltpu.VMEM((width, rows), jnp.bfloat16),
            pltpu.VMEM((width, rows), jnp.bfloat16),
            pltpu.VMEM((grid_rows, rows, width), jnp.bfloat16),
            pltpu.VMEM((grid_rows, rows, width), jnp.bfloat16),
        ],
        compiler_params=pltpu.CompilerParams(vmem_limit_bytes=48 * 2**20),
        name="product",
    )(row_panel, col_panel)


def per_device(aux_slab, gaps, frequency):
    devices = lax.axis_size("row")
    bit_count = devices.bit_length() - 1
    grid_cols = 2 ** (bit_count // 2)
    grid_rows = devices // grid_cols
    weights = 2.0 * gaps / (gaps * gaps + frequency[0] * frequency[0])
    block = aux_slab * jnp.sqrt(weights)[:, None]
    col_panel, row_panel = gather_panels(block, grid_rows, grid_cols)
    return product(row_panel, col_panel)[None]


def solution(mesh):
    in_specs = (P(None, "row"), P(), P())
    out_specs = P("row", None, None)
    return jax.shard_map(
        per_device, mesh=mesh, in_specs=in_specs, out_specs=out_specs, check_vma=False
    )
```

```python
import functools
import jax
import jax.numpy as jnp
from jax import lax
from jax.experimental import pallas as pl
from jax.experimental.pallas import tpu as pltpu
from jax.sharding import PartitionSpec as P

MESH = pl.DeviceIdType.MESH
CHUNKS = 4
LAG = 2


def slot_at(place, grid_rows):
    place = lax.rem(place + 2 * grid_rows, grid_rows)
    return jnp.where(place < grid_rows // 2, 2 * place, 2 * (grid_rows - 1 - place) + 1)


def place_of(slot, grid_rows):
    return jnp.where(lax.rem(slot, 2) == 0, slot // 2, grid_rows - 1 - slot // 2)


def flipped(value, weight):
    return value + weight * (1 - 2 * lax.rem(value // weight, 2))


def coupling_kernel(
    grid_rows, grid_cols, block_ref, scale_ref, out_ref, col_ref, row_ref, row_high, row_low, col_high, col_low,
    tile_ref, own_sem, tile_sem, ring_send, ring_recv, row_send, row_recv
):
    bits = grid_cols.bit_length() - 1
    half = grid_rows // 2
    depth = block_ref.shape[0] // CHUNKS
    width = block_ref.shape[1]
    spread = grid_rows // grid_cols
    me = lax.axis_index("row")
    grid_row, grid_col = me // grid_cols, lax.rem(me, grid_cols)
    source_col = lax.rem(grid_row, grid_cols)
    place = place_of(grid_row, grid_rows)
    right = slot_at(place + 1, grid_rows) * grid_cols + grid_col
    left = slot_at(place - 1, grid_rows) * grid_cols + grid_col
    neighbours = (right, left)
    differs = [
        lax.rem(grid_col // 2**bit + source_col // 2**bit, 2) for bit in range(bits)
    ]
    none_below = [jnp.int32(1)]
    for bit in range(bits):
        none_below.append(none_below[-1] * (1 - differs[bit]))
    is_source = none_below[bits] == 1
    passes = [none_below[bit + 1] == 1 for bit in range(bits)]
    children = [grid_row * grid_cols + flipped(grid_col, 2**bit) for bit in range(bits)]

    own_copy = pltpu.make_async_copy(block_ref, col_ref.at[grid_row], own_sem)
    own_copy.start()
    barrier = pltpu.get_barrier_semaphore()
    for dev in (right, left):
        pl.semaphore_signal(barrier, inc=1, device_id=(dev,), device_id_type=MESH)
    for step in range(1, grid_cols):
        dev = grid_row * grid_cols + lax.rem(grid_col + step, grid_cols)
        pl.semaphore_signal(barrier, inc=1, device_id=(dev,), device_id_type=MESH)
    own_copy.wait()
    col_ref[grid_row] = col_ref[grid_row] * scale_ref[...]
    pl.semaphore_wait(barrier, 1 + grid_cols)

    def chunk(ref, slot, part):
        return ref.at[slot, pl.ds(pl.multiple_of(part * depth, 8), depth), :]

    def ring_copy(way, slot, step, part):
        return pltpu.make_async_remote_copy(
            src_ref=chunk(col_ref, slot, part),
            dst_ref=chunk(col_ref, slot, part),
            send_sem=ring_send.at[way, step, part],
            recv_sem=ring_recv.at[way, step, part],
            device_id=(neighbours[way],),
            device_id_type=MESH,
        )

    def row_copy(ref, slot, row_slot, part, bit):
        return pltpu.make_async_remote_copy(
            src_ref=chunk(ref, slot, part),
            dst_ref=chunk(row_ref, row_slot, part),
            send_sem=row_send.at[bit, row_slot, part],
            recv_sem=row_recv.at[row_slot, part],
            device_id=(children[bit],),
            device_id_type=MESH,
        )

    def event(index):
        step, turn = index // CHUNKS, lax.rem(index, CHUNKS)
        ways = []
        for way, part in ((0, turn), (1, CHUNKS - 1 - turn)):
            slot = slot_at(place - step if way == 0 else place + step, grid_rows)
            sends = (step < half - 1) | ((step == half - 1) & (turn < CHUNKS // 2))
            counts = (step > 0) if way == 1 else (step >= 0)
            in_row = counts & (lax.rem(slot, spread) == grid_row // grid_cols)
            ways.append((way, part, slot, slot // spread, step, sends, in_row))
        return ways

    total = half * CHUNKS + CHUNKS // 2

    def arrive(index):
        for way, part, slot, row_slot, step, sends, in_row in event(index):

            @pl.when(step > 0)
            def _():
                ring_copy(way, slot, step - 1, part).wait_recv()

            @pl.when(sends)
            def _():
                ring_copy(way, slot, step, part).start()

            @pl.when(in_row & is_source)
            def _():
                for bit in range(bits - 1, -1, -1):
                    row_copy(col_ref, slot, row_slot, part, bit).start()

    def relay(index):
        for way, part, slot, row_slot, step, sends, in_row in event(index):

            @pl.when(in_row & jnp.logical_not(is_source))
            def _():
                row_copy(col_ref, slot, row_slot, part, 0).wait_recv()
                for bit in range(bits - 1, -1, -1):

                    @pl.when(passes[bit])
                    def _():
                        row_copy(row_ref, row_slot, row_slot, part, bit).start()

    def drain(index):
        for way, part, slot, row_slot, step, sends, in_row in event(index):

            @pl.when(sends)
            def _():
                ring_copy(way, slot, step, part).wait_send()

            for bit in range(bits):

                @pl.when(in_row & passes[bit])
                def _():
                    row_copy(col_ref, slot, row_slot, part, bit).wait_send()

    def distance(slot):
        ahead = lax.rem(place_of(slot, grid_rows) - place + grid_rows, grid_rows)
        return jnp.minimum(ahead, grid_rows - ahead)

    def row_origin(u):
        return u * spread + grid_row // grid_cols

    def prepare_row(u, ref, slot):
        high, low = split(ref[slot].T)
        row_high[u] = high
        row_low[u] = low

    def prepare(level):
        @pl.loop(0, grid_rows)
        def _(v):
            @pl.when(distance(v) == level)
            def _():
                high, low = split(col_ref[v])
                col_high[v] = high
                col_low[v] = low

        @pl.loop(0, grid_cols)
        def _(u):
            new = distance(row_origin(u)) == level

            @pl.when(new & is_source)
            def _():
                prepare_row(u, col_ref, row_origin(u))

            @pl.when(new & jnp.logical_not(is_source))
            def _():
                prepare_row(u, row_ref, u)

    def tile_copy(u, v, buffer):
        return pltpu.make_async_copy(
            tile_ref.at[buffer],
            out_ref.at[
                pl.ds(pl.multiple_of(u * width, width), width), pl.ds(pl.multiple_of(v * width, width), width)
            ],
            tile_sem.at[buffer],
        )

    def dot(first, second):
        return jnp.dot(first, second, preferred_element_type=jnp.float32)

    def multiply(level, turn, count):
        def pair(number, count):
            u, v = number // grid_rows, lax.rem(number, grid_rows)
            due = jnp.maximum(distance(v), distance(row_origin(u))) == level
            due = due & (lax.rem(u + v, CHUNKS) == turn)
            buffer = lax.rem(count, 2)

            @pl.when(due)
            def _():
                @pl.when(count >= 2)
                def _():
                    tile_copy(u, v, buffer).wait()

                high = row_high[u]
                tile_ref[buffer] = dot(high, col_high[v]) + (dot(high, col_low[v]) + dot(row_low[u], col_high[v]))

                @pl.when(u * grid_rows + grid_row == v * grid_cols + grid_col)
                def _():
                    lines = lax.broadcasted_iota(jnp.int32, (width, width), 0)
                    lanes = lax.broadcasted_iota(jnp.int32, (width, width), 1)
                    tile_ref[buffer] += (lines == lanes).astype(jnp.float32)

                tile_copy(u, v, buffer).start()

            return count + due.astype(jnp.int32)

        return lax.fori_loop(0, grid_cols * grid_rows, pair, count)

    wait_levels = LAG + CHUNKS - 1

    def body(index, count):
        @pl.when(index < total)
        def _():
            arrive(index)

        @pl.when((index >= LAG) & (index < total + LAG))
        def _():
            relay(index - LAG)

        ready = index >= wait_levels
        level = jnp.where(ready, (index - wait_levels) // CHUNKS, -1)
        turn = lax.rem(index + CHUNKS * wait_levels - wait_levels, CHUNKS)

        @pl.when(ready & (turn == 0))
        def _():
            prepare(level)

        return multiply(level, turn, count)

    lax.fori_loop(0, wait_levels + (half + 1) * CHUNKS, body, jnp.int32(0))

    for buffer in range(2):
        tile_copy(0, 0, buffer).wait()

    @pl.loop(0, total)
    def _(index):
        drain(index)


def split(value):
    high = value.astype(jnp.bfloat16)
    return high, (value - high.astype(jnp.float32)).astype(jnp.bfloat16)


def coupling_tile(block, scale, grid_rows, grid_cols):
    bits = grid_cols.bit_length() - 1
    half = grid_rows // 2
    rows, width = block.shape
    return pl.pallas_call(
        functools.partial(coupling_kernel, grid_rows, grid_cols),
        out_shape=jax.ShapeDtypeStruct((grid_cols * width, grid_rows * width), jnp.float32),
        in_specs=[pl.BlockSpec(memory_space=pl.ANY), pl.BlockSpec(memory_space=pltpu.VMEM)],
        out_specs=pl.BlockSpec(memory_space=pl.ANY),
        scratch_shapes=[
            pltpu.VMEM((grid_rows, rows, width), jnp.float32),
            pltpu.VMEM((grid_cols, rows, width), jnp.float32),
            pltpu.VMEM((grid_cols, width, rows), jnp.bfloat16),
            pltpu.VMEM((grid_cols, width, rows), jnp.bfloat16),
            pltpu.VMEM((grid_rows, rows, width), jnp.bfloat16),
            pltpu.VMEM((grid_rows, rows, width), jnp.bfloat16),
            pltpu.VMEM((2, width, width), jnp.float32),
            pltpu.SemaphoreType.DMA,
            pltpu.SemaphoreType.DMA((2,)),
            pltpu.SemaphoreType.DMA((2, half, CHUNKS)),
            pltpu.SemaphoreType.DMA((2, half, CHUNKS)),
            pltpu.SemaphoreType.DMA((bits, grid_cols, CHUNKS)),
            pltpu.SemaphoreType.DMA((grid_cols, CHUNKS)),
        ],
        compiler_params=pltpu.CompilerParams(
            collective_id=0, has_side_effects=True, vmem_limit_bytes=56 * 2**20
        ),
        name="coupling_tile",
    )(block, scale)


def per_device(aux_slab, gaps, frequency):
    devices = lax.axis_size("row")
    bit_count = devices.bit_length() - 1
    grid_cols = 2 ** (bit_count // 2)
    grid_rows = devices // grid_cols
    weights = 2.0 * gaps / (gaps * gaps + frequency[0] * frequency[0])
    return coupling_tile(aux_slab, jnp.sqrt(weights)[:, None], grid_rows, grid_cols)[None]


def solution(mesh):
    in_specs = (P(None, "row"), P(), P())
    out_specs = P("row", None, None)
    return jax.shard_map(
        per_device, mesh=mesh, in_specs=in_specs, out_specs=out_specs, check_vma=False
    )
```
